512 devices in a mesh: geo: 128 (over z, y, core), rep: 4 (over x).
Axes of the slice: x: 4, y: 8, z: 8, core: 2. Of those that a mesh axis runs over, the one named last changes fastest.
Arguments:
- base: float32 [1048576], P(('geo', 'rep')), may hold values from 0.5 to 2
- job_res: int32 [1048576], P(('geo', 'rep')), may hold values from 0 to 255
- job_slot: int32 [1048576], P(('geo', 'rep')), may hold values from 0 to 4095
- job_cell: int32 [1048576], P(('geo', 'rep')), may hold values from 0 to 29
- needed: int32 [128, 128, 1], P('geo'), may hold values from 0 to 7
- lam_res: float32 [30, 32768], P(None, 'geo'), may hold values from -2 to 2
- lam_work: float32 [30, 32768], P(None, 'geo'), may hold values from -2 to 2
- target_res: float32 [30, 32768], P(None, 'geo'), may hold values from 0.3 to 3
- target_work: float32 [30, 32768], P(None, 'geo'), may hold values from 0.3 to 3
Outputs:
- step_res: float32 [30, 32768], P(None, 'geo')
- step_work: float32 [30, 32768], P(None, 'geo')
- resid_res: float32 [30, 32768], P(None, 'geo')
- resid_work: float32 [30, 32768], P(None, 'geo')
The draws below stay inside these ranges and needn't reach their ends.
Inputs may be any that keep to these rules, and one draw needn't show every extreme that they name: needed[g, p, k] is a block of owner p's tracts; block b covers that owner's local tracts b * 32 to b * 32 + 31.
All inputs are finite; a program needn't handle non-finite values.
Results may differ from the reference program's by a relative error of at most 0.0003.
Values sent between devices are 32-bit elements; how exact they have to be, the bound alone decides.
A program may use at most 64 MiB of HBM per device.

```python
import math
import jax
import jax.numpy as jnp

CELLS = 30
BLK = 32
CAP = 1
ITERS = 3
TR_DEV = 256
JOB_DEV = 2048
BLOCKS = 8
TRACTS = 32768
SLOTS = 4096
JOBS = 1048576
N_GEO = 128
N_REP = 4


def set_ends(result, key, least, high):
    spot = [jax.random.randint(jax.random.fold_in(key, axis), (), 0, length) for axis, length in enumerate(result.shape)]
    longest = result.shape.index(max(result.shape))
    beside = spot[:longest] + [(spot[longest] + 1) % result.shape[longest]] + spot[longest + 1:]
    return result.at[tuple(spot)].set(least).at[tuple(beside)].set(high)


def block_scale(key, shape, pieces, low, top_value):
    def one(position, blocks):
        heights = jax.random.uniform(jax.random.fold_in(jax.random.fold_in(key, 6), position), (blocks,), jnp.float32, low / len(pieces), top_value / len(pieces))
        return jnp.repeat(jnp.exp(heights), shape[position] // blocks).reshape((-1,) + (1,) * (len(shape) - position - 1))

    level = one(*pieces[0])
    for cut in pieces[1:]:
        level = level * one(*cut)
    return level


def normal_values(key, extent, width, most, cuts=(), kind=jnp.bfloat16):
    drawn = width * jax.random.normal(key, extent, jnp.float32)
    if cuts:
        drawn = drawn * block_scale(key, extent, cuts, -0.22, 0.18)
    return jnp.clip(drawn, -most, most).astype(kind)


def setup_inputs(seed: int = 0) -> dict:
    streams_of = jax.random.split(jax.random.key(seed), 10)
    return {
        "base": jnp.clip(jnp.exp(math.log(2.0) - 1.3862944 * jax.random.uniform(streams_of[0], (JOBS,), jnp.float32) ** block_scale(streams_of[0], (JOBS,), ((0, 512),), -0.2, 0.2)), 0.5, 2.0),
        "job_res": set_ends(jax.random.randint(streams_of[1], (JOBS,), 0, TR_DEV), jax.random.fold_in(streams_of[1], 1), 0, TR_DEV - 1).astype(jnp.int32),
        "job_slot": set_ends(jax.random.randint(streams_of[2], (JOBS,), 0, SLOTS), jax.random.fold_in(streams_of[2], 1), 0, SLOTS - 1).astype(jnp.int32),
        "job_cell": set_ends(jax.random.randint(streams_of[3], (JOBS,), 0, CELLS), jax.random.fold_in(streams_of[3], 1), 0, CELLS - 1).astype(jnp.int32),
        "needed": set_ends(jax.random.randint(streams_of[4], (N_GEO, N_GEO, CAP), 0, BLOCKS), jax.random.fold_in(streams_of[4], 1), 0, BLOCKS - 1).astype(jnp.int32),
        "lam_res": normal_values(streams_of[5], (CELLS, TRACTS), 0.3, 2.0, ((1, 128),), jnp.float32),
        "lam_work": normal_values(streams_of[6], (CELLS, TRACTS), 0.3, 2.0, ((1, 128),), jnp.float32),
        "target_res": jnp.clip(jnp.exp(math.log(3.0) - 2.3025851 * jax.random.uniform(streams_of[7], (CELLS, TRACTS), jnp.float32) ** block_scale(streams_of[7], (CELLS, TRACTS), ((1, 128),), -0.2, 0.2)), 0.3, 3.0),
        "target_work": jnp.clip(jnp.exp(math.log(3.0) - 2.3025851 * jax.random.uniform(streams_of[8], (CELLS, TRACTS), jnp.float32) ** block_scale(streams_of[8], (CELLS, TRACTS), ((1, 128),), -0.2, 0.2)), 0.3, 3.0),
    }


RIDGE = 0.5


def reference(base, job_res, job_slot, job_cell, needed, lam_res, lam_work, target_res, target_work):
    tracts = lam_res.shape[1]
    group = (jnp.arange(JOBS, dtype=jnp.int32) // (JOB_DEV * N_REP)).astype(jnp.int32)
    owner = (job_slot // (CAP * BLK)).astype(jnp.int32)
    within = ((job_slot // BLK) % CAP).astype(jnp.int32)
    block = needed[group, owner, within].astype(jnp.int32)
    res_tract = group * TR_DEV + job_res
    work_tract = owner * TR_DEV + block * BLK + job_slot % BLK
    res_index = (job_cell * tracts + res_tract).astype(jnp.int32)
    work_index = (job_cell * tracts + work_tract).astype(jnp.int32)
    weight = base * jnp.exp(lam_res.reshape(-1)[res_index] + lam_work.reshape(-1)[work_index])

    def totals(values):
        res_part = jax.ops.segment_sum(values, res_index, num_segments=CELLS * tracts).reshape(CELLS, tracts)
        work_part = jax.ops.segment_sum(values, work_index, num_segments=CELLS * tracts).reshape(CELLS, tracts)
        return res_part, work_part

    def inner(a_res, a_work, b_res, b_work):
        return jnp.sum(a_res * b_res) + jnp.sum(a_work * b_work)

    total_res, total_work = totals(weight)
    resid_res = -(total_res - target_res)
    resid_work = -(total_work - target_work)
    step_res = jnp.zeros_like(resid_res)
    step_work = jnp.zeros_like(resid_work)
    dir_res, dir_work = resid_res, resid_work
    norm_now = inner(resid_res, resid_work, resid_res, resid_work)
    for turn in range(ITERS):
        along = dir_res.reshape(-1)[res_index] + dir_work.reshape(-1)[work_index]
        image_res, image_work = totals(weight * along)
        image_res = image_res + RIDGE * dir_res
        image_work = image_work + RIDGE * dir_work
        alpha = norm_now / inner(dir_res, dir_work, image_res, image_work)
        step_res = step_res + alpha * dir_res
        step_work = step_work + alpha * dir_work
        resid_res = resid_res - alpha * image_res
        resid_work = resid_work - alpha * image_work
        norm_next = inner(resid_res, resid_work, resid_res, resid_work)
        dir_res = resid_res + (norm_next / norm_now) * dir_res
        dir_work = resid_work + (norm_next / norm_now) * dir_work
        norm_now = norm_next
    return (step_res, step_work, resid_res, resid_work)
```

```python
import functools

import jax
import jax.numpy as jnp
from jax import lax
from jax.experimental import pallas as pl
from jax.experimental.pallas import tpu as pltpu
from jax.sharding import PartitionSpec as P

BLK = 32
ITERS = 3
RIDGE = 0.5
MESH = pl.DeviceIdType.MESH
LANES = 128
PART = 8
CAP = 48
STEEP = 128.0
FLAT = 1e-3
BF = jnp.bfloat16
F32 = jnp.float32


def gather(table, index, rows):
    high = index >> 7
    low = index & 127
    out = jnp.zeros(index.shape, F32)
    for row in range(rows):
        for half in range(2):
            line = table[row : row + 1, half * LANES : (half + 1) * LANES]
            line = jnp.broadcast_to(line, index.shape)
            out = jnp.where(high == 2 * row + half, jnp.take_along_axis(line, low, axis=1), out)
    return out


def share_kernel(
    n_rep, base, res, slot, cell, needed, lam_res, lam_work, t_res, t_work,
    jobs, parts, send, recv, wide, send_sem, recv_sem,
):
    g, r = lax.axis_index("geo"), lax.axis_index("rep")
    barrier = pltpu.get_barrier_semaphore()
    for i in range(1, n_rep):
        pl.semaphore_signal(
            barrier, inc=1, device_id=(g, lax.rem(r + i, n_rep)), device_id_type=MESH
        )
    cells = lam_res.shape[0]
    n = base.shape[0]
    c = cell[...]
    s = slot[...]
    p = s >> 5
    block = jnp.take_along_axis(jnp.broadcast_to(needed[...], s.shape), p, axis=1)
    work = c * 256 + block * BLK + (s & (BLK - 1))
    home = c * 256 + res[...]
    u = base[...] * jnp.exp(gather(lam_res[...], home, cells))
    send[0:n, :] = u
    send[n : 2 * n, :] = p.astype(F32)
    send[2 * n : 3 * n, :] = work.astype(F32)
    send[3 * n : 4 * n, :] = home.astype(F32)
    for k, table in enumerate((lam_work, t_res, t_work)):
        wide[k] = jnp.zeros(wide.shape[1:], F32)
        wide[k, 0:cells, :] = table[...]
        parts[k] = wide[k, pl.ds(pl.multiple_of(r * PART, PART), PART), :]
    pl.semaphore_wait(barrier, n_rep - 1)
    copies = []
    for i in range(1, n_rep):
        copy = pltpu.make_async_remote_copy(
            src_ref=send,
            dst_ref=recv.at[r],
            send_sem=send_sem.at[i - 1],
            recv_sem=recv_sem.at[i - 1],
            device_id=(g, lax.rem(r + i, n_rep)),
            device_id_type=MESH,
        )
        copy.start()
        copies.append(copy)
    recv[r] = send[...]
    for copy in copies:
        copy.wait()
    for q in range(n_rep):
        for f in range(4):
            jobs[f, q * n : (q + 1) * n, :] = recv[q, f * n : (f + 1) * n, :]


def split(x):
    high = x.astype(BF).astype(F32)
    return high, x - high


def newton_kernel(
    n_geo, n_rep, jobs, parts, o_sr, o_sw, o_rr, o_rw, o_flag,
    ohp, pre, rank, fields, place, oht_r, oht_w, left, send, recv, xbuf,
    send_sem, recv_sem, xsend_sem, xrecv_sem,
):
    g, r = lax.axis_index("geo"), lax.axis_index("rep")
    barrier = pltpu.get_barrier_semaphore()

    def greet(i, carry):
        pl.semaphore_signal(
            barrier, inc=1, device_id=(lax.rem(g + i, n_geo), r), device_id_type=MESH
        )
        return carry

    lax.fori_loop(1, n_geo, greet, 0)
    for i in range(1, n_rep):
        pl.semaphore_signal(
            barrier, inc=1, device_id=(g, lax.rem(r + i, n_rep)), device_id_type=MESH
        )

    rows = jobs.shape[1]
    chunks = rows // 2
    u_all = jobs[0]
    work_all = jobs[2].astype(jnp.int32)
    home_all = jobs[3].astype(jnp.int32)
    local = (work_all >> 8) - r * PART
    inside = (local >= 0) & (local < PART)
    owner = jnp.where(inside, jobs[1].astype(jnp.int32), 2 * LANES)
    peers = lax.broadcasted_iota(jnp.int32, (LANES, 2 * LANES), 0)

    def pair(x, c):
        return jnp.concatenate([x[2 * c : 2 * c + 1, :], x[2 * c + 1 : 2 * c + 2, :]], axis=1)

    before = lax.broadcasted_iota(jnp.int32, (2 * LANES, 2 * LANES), 0)
    after = lax.broadcasted_iota(jnp.int32, (2 * LANES, 2 * LANES), 1)
    upto = jnp.where(before <= after, 1.0, 0.0).astype(BF)
    for c in range(chunks):
        span = slice(c * 256, (c + 1) * 256)
        hot = jnp.where(pair(owner, c) == peers, 1.0, 0.0)
        ohp[:, span] = hot.astype(BF)
    for c in range(chunks):
        span = slice(c * 256, (c + 1) * 256)
        pre[:, span] = jnp.dot(ohp[:, span], upto, preferred_element_type=F32)
    so_far = jnp.zeros((LANES, 1), F32)
    most = jnp.zeros((1, 256), F32)
    u_1 = u_all.astype(BF).astype(F32)
    u_2 = (u_all - u_1).astype(BF).astype(F32)
    u_3 = u_all - u_1 - u_2
    kinds = (
        u_1,
        u_2,
        u_3,
        local.astype(F32),
        (work_all & 255).astype(F32),
        (home_all & 255).astype(F32),
    )
    steps = lax.broadcasted_iota(jnp.int32, (CAP, 256), 0).astype(F32)
    for c in range(chunks):
        span = slice(c * 256, (c + 1) * 256)
        here = pre[:, span]
        place_c = jnp.sum(ohp[:, span].astype(F32) * (here + so_far), axis=0, keepdims=True) - 1.0
        so_far = so_far + here[:, 255:256]
        most = jnp.maximum(most, place_c)
        spot = place_c == steps
        for f, kind in enumerate(kinds):
            fields[f * CAP : (f + 1) * CAP, span] = jnp.where(spot, pair(kind, c), 0.0).astype(BF)
    place[...] = lax.dot_general(
        fields[...], ohp[...], (((1,), (1,)), ((), ())), preferred_element_type=F32
    )
    u_g = place[0:CAP, :] + place[CAP : 2 * CAP, :] + place[2 * CAP : 3 * CAP, :]
    cell_g = place[3 * CAP : 4 * CAP, :]
    work_g = cell_g * 256.0 + place[4 * CAP : 5 * CAP, :]
    res_g = place[5 * CAP : 6 * CAP, :]
    home_g = (cell_g * 256.0 + res_g).astype(jnp.int32)
    cell_g = cell_g.astype(jnp.int32)

    pad = jnp.zeros((LANES - 2 * CAP, LANES), F32)

    def launch(k, first, second):
        whole = jnp.concatenate([first, second, pad], axis=0)
        send[k] = jnp.transpose(whole).reshape(LANES, 1, LANES)

        def go(i, carry):
            peer = lax.rem(g + i, n_geo)
            pltpu.make_async_remote_copy(
                src_ref=send.at[k, peer],
                dst_ref=recv.at[k, g],
                send_sem=send_sem.at[k],
                recv_sem=recv_sem.at[k],
                device_id=(peer, r),
                device_id_type=MESH,
            ).start()
            return carry

        lax.fori_loop(1, n_geo, go, 0, unroll=True if n_geo < 8 else 1)
        recv[k, g] = send[k, g]

    def everything(k):
        return pltpu.make_async_remote_copy(
            src_ref=send.at[k, pl.ds(0, n_geo - 1)],
            dst_ref=recv.at[k, pl.ds(0, n_geo - 1)],
            send_sem=send_sem.at[k],
            recv_sem=recv_sem.at[k],
            device_id=(g, r),
            device_id_type=MESH,
        )

    def arrive(k):
        everything(k).wait_recv()
        return recv[k].reshape(LANES, LANES)

    tracts = lax.broadcasted_iota(jnp.int32, (LANES, 256), 1).astype(F32)

    def columns(oht, numbers):
        for k in range(CAP):
            hot = jnp.where(numbers[:, k : k + 1] == tracts, 1.0, 0.0)
            oht[k * LANES : (k + 1) * LANES, :] = hot.astype(BF)

    lines = lax.broadcasted_iota(jnp.int32, (PART, LANES), 0)

    def scatter(values, cell, oht):
        pieces = [piece for value in values for piece in split(value)]
        for k in range(CAP):
            mine = cell[k : k + 1, :] == lines
            stack = [jnp.where(mine, piece[k : k + 1, :], 0.0) for piece in pieces]
            left[0 : PART * len(pieces), k * LANES : (k + 1) * LANES] = jnp.concatenate(
                stack, axis=0
            ).astype(BF)
        out = jnp.dot(left[0 : PART * len(pieces), :], oht[...], preferred_element_type=F32)
        return [
            out[2 * v * PART : (2 * v + 1) * PART] + out[(2 * v + 1) * PART : (2 * v + 2) * PART]
            for v in range(len(values))
        ]

    pl.semaphore_wait(barrier, n_geo - 1 + n_rep - 1)
    launch(0, u_g, work_g)
    columns(oht_r, jnp.transpose(jnp.concatenate([res_g, jnp.zeros((LANES - CAP, LANES), F32)], axis=0)))

    got = arrive(0)
    flat = jnp.transpose(got)
    u_o = flat[0:CAP]
    work_o = flat[CAP : 2 * CAP].astype(jnp.int32)
    cell_o = work_o >> 8
    columns(oht_w, (got[:, CAP : 2 * CAP].astype(jnp.int32) & 255).astype(F32))
    w_o = u_o * gather(jnp.exp(parts[0]), work_o, PART)
    [sum_w] = scatter([w_o], cell_o, oht_w)
    diag_w = sum_w + RIDGE
    b0 = parts[2] - sum_w
    launch(1, w_o, gather(b0, work_o, PART))

    flat = jnp.transpose(arrive(1))
    w_g = flat[0:CAP]
    sum_r, bb0 = scatter([w_g, w_g * flat[CAP : 2 * CAP]], cell_g, oht_r)
    diag_r = sum_r + RIDGE
    a0 = parts[1] - sum_r
    a1 = diag_r * a0 + bb0
    launch(2, w_g * gather(a0, home_g, PART), w_g * gather(a1, home_g, PART))

    flat = jnp.transpose(arrive(2))
    ba0, ba1 = scatter([flat[0:CAP], flat[CAP : 2 * CAP]], cell_o, oht_w)
    b1 = diag_w * b0 + ba0
    b2 = diag_w * b1 + ba1
    launch(3, w_o * gather(b1, work_o, PART), w_o * gather(b2, work_o, PART))

    flat = jnp.transpose(arrive(3))
    bb1, bb2 = scatter([flat[0:CAP], flat[CAP : 2 * CAP]], cell_g, oht_r)
    a2 = diag_r * a1 + bb1
    a3 = diag_r * a2 + bb2

    def line(x):
        x = x[:, 0:LANES] + x[:, LANES : 2 * LANES]
        return jnp.sum(x, axis=0, keepdims=True)

    steep = jnp.maximum(jnp.max(sum_r), jnp.max(sum_w))
    bad = jnp.where(jnp.logical_or(steep > STEEP, jnp.max(most) >= CAP), 1.0, 0.0)
    table = jnp.concatenate(
        [
            line(a0 * a0 + b0 * b0),
            line(a0 * a1 + b0 * b1),
            line(a1 * a1 + b1 * b1),
            line(a1 * a2 + b1 * b2),
            line(a2 * a2 + b2 * b2),
            line(a2 * (a3 + bb2) + diag_w * b2 * b2),
            jnp.full((1, LANES), bad, F32),
            jnp.zeros((1, LANES), F32),
        ],
        axis=0,
    )
    table = jnp.broadcast_to(jnp.sum(table, axis=1, keepdims=True), (8, LANES))
    launch(
        4,
        w_g * gather(a2, home_g, PART),
        jnp.concatenate([table, jnp.zeros((CAP - 8, LANES), F32)], axis=0),
    )

    early = 7 * PART
    for v, vector in enumerate((a0, a1, a2, a3, b0, b1, b2)):
        xbuf[r, v * PART : (v + 1) * PART, :] = vector

    def across(lo, hi, which):
        copies = []
        for i in range(1, n_rep):
            copy = pltpu.make_async_remote_copy(
                src_ref=xbuf.at[r, pl.ds(lo, hi - lo)],
                dst_ref=xbuf.at[r, pl.ds(lo, hi - lo)],
                send_sem=xsend_sem.at[which, i - 1],
                recv_sem=xrecv_sem.at[which, i - 1],
                device_id=(g, lax.rem(r + i, n_rep)),
                device_id_type=MESH,
            )
            copy.start()
            copies.append(copy)
        return copies

    first = across(0, early, 0)

    flat = jnp.transpose(arrive(4))
    [ba2] = scatter([flat[0:CAP]], cell_o, oht_w)
    b3 = diag_w * b2 + ba2
    xbuf[r, early : early + PART, :] = b3
    xbuf[r, early + PART : early + 2 * PART, :] = jnp.broadcast_to(
        jnp.sum(flat[CAP : CAP + 8], axis=1, keepdims=True), (8, 256)
    )
    last = across(early, early + 2 * PART, 1)
    for copy in first + last:
        copy.wait()
    for k in range(5):
        everything(k).wait_send()

    sums = xbuf[0, early + PART : early + 2 * PART, :]
    for q in range(1, n_rep):
        sums = sums + xbuf[q, early + PART : early + 2 * PART, :]
    m = [sums[i : i + 1, :] for i in range(7)]

    def form(x, shift):
        n = len(x)
        total = None
        for s in range(2 * n - 1):
            part = None
            for i in range(max(0, s - n + 1), min(n - 1, s) + 1):
                term = x[i] * x[s - i]
                part = term if part is None else part + term
            part = part * m[s + shift]
            total = part if total is None else total + part
        return total

    one = jnp.ones((1, 256), F32)
    rc, pc, xc = [one], [one], []
    norm = m[0]
    for turn in range(ITERS):
        alpha = norm / form(pc, 1)
        xc = [x + alpha * p for x, p in zip(xc, pc)] + [alpha * pc[-1]]
        image = [-alpha * p for p in pc]
        rc = [rc[0]] + [x + y for x, y in zip(rc[1:], image[:-1])] + [image[-1]]
        if turn < ITERS - 1:
            new = form(rc, 0)
            beta = new / norm
            pc = [x + beta * p for x, p in zip(rc[:-1], pc)] + [rc[-1]]
            norm = new
    good = jnp.logical_and(m[6] == 0.0, norm > FLAT * m[0])
    o_flag[...] = jnp.broadcast_to(jnp.where(good, 0.0, 1.0)[:, 0:LANES], (8, LANES))
    cells = o_sr.shape[0]
    for q in range(n_rep):
        lo, hi = q * PART, min((q + 1) * PART, cells)
        for side, o_step, o_resid in ((0, o_sr, o_rr), (1, o_sw, o_rw)):
            k = [
                xbuf[q, (4 * side + i) * PART : (4 * side + i) * PART + hi - lo, :]
                for i in range(4)
            ]
            o_step[lo:hi, :] = xc[0] * k[0] + xc[1] * k[1] + xc[2] * k[2]
            o_resid[lo:hi, :] = k[0] + rc[1] * k[1] + rc[2] * k[2] + rc[3] * k[3]


def general(base, job_res, job_slot, job_cell, needed, lam_res, lam_work, target_res, target_work):
    cells, tracts_dev = lam_res.shape
    blocks_dev = tracts_dev // BLK
    requests = lax.all_to_all(needed[0], "geo", split_axis=0, concat_axis=0, tiled=True)
    sources, listed = requests.shape
    hot = requests[:, :, None] == jnp.arange(blocks_dev, dtype=jnp.int32)[None, None, :]
    onehot = hot.astype(jnp.float32)
    slot_shape = (sources, listed, cells, BLK)
    slot_count = sources * listed * cells * BLK
    res_index = job_cell * tracts_dev + job_res
    work_index = (job_slot // BLK * cells + job_cell) * BLK + job_slot % BLK

    def serve(table):
        blocks = table.reshape(cells, blocks_dev, BLK).transpose(1, 0, 2)
        out = jnp.zeros(slot_shape, jnp.float32)
        for b in range(blocks_dev):
            out = jnp.where(hot[:, :, b, None, None], blocks[b][None, None], out)
        return out

    def pick(fetched):
        return fetched.reshape(-1)[work_index]

    def fold(arrived):
        return jnp.einsum("skb,skcx->cbx", onehot, arrived, precision=lax.Precision.HIGHEST)

    def totals(values):
        res_part = jax.ops.segment_sum(values, res_index, num_segments=cells * tracts_dev).reshape(
            cells, tracts_dev
        )
        work_part = jax.ops.segment_sum(values, work_index, num_segments=slot_count).reshape(
            slot_shape
        )
        arrived = lax.all_to_all(work_part, "geo", split_axis=0, concat_axis=0, tiled=True)
        folded = fold(arrived)
        return lax.psum((res_part, folded.reshape(cells, tracts_dev)), "rep")

    def squares(part_res, part_work):
        local = jnp.sum(part_res * part_res) + jnp.sum(part_work * part_work)
        return lax.psum(local, "geo")

    def fetch(table):
        return lax.all_to_all(serve(table), "geo", split_axis=0, concat_axis=0, tiled=True)

    weight = base * jnp.exp(lam_res.reshape(-1)[res_index] + pick(fetch(lam_work)))
    total_res, total_work = totals(weight)
    resid_res = -(total_res - target_res)
    resid_work = -(total_work - target_work)
    zero = jnp.zeros_like(resid_res)
    norm = squares(resid_res, resid_work)

    def turn(_, state):
        step_res, step_work, resid_res, resid_work, dir_res, dir_work, norm_now = state
        along = dir_res.reshape(-1)[res_index] + pick(fetch(dir_work))
        image_res, image_work = totals(weight * along)
        image_res = image_res + RIDGE * dir_res
        image_work = image_work + RIDGE * dir_work
        local_curv = jnp.sum(dir_res * image_res) + jnp.sum(dir_work * image_work)
        alpha = norm_now / lax.psum(local_curv, "geo")
        step_res = step_res + alpha * dir_res
        step_work = step_work + alpha * dir_work
        resid_res = resid_res - alpha * image_res
        resid_work = resid_work - alpha * image_work
        norm_next = squares(resid_res, resid_work)
        dir_res = resid_res + norm_next / norm_now * dir_res
        dir_work = resid_work + norm_next / norm_now * dir_work
        return step_res, step_work, resid_res, resid_work, dir_res, dir_work, norm_next

    state = (zero, zero, resid_res, resid_work, resid_res, resid_work, norm)
    return lax.fori_loop(0, ITERS, turn, state)[:4]


def body(n_geo, n_rep, *args):
    base, job_res, job_slot, job_cell, needed, lam_res, lam_work, target_res, target_work = args
    n = base.shape[0] // LANES
    cells, tracts = lam_res.shape
    vmem = pl.BlockSpec(memory_space=pltpu.VMEM)
    dma = pltpu.SemaphoreType.DMA
    jobs, parts = pl.pallas_call(
        functools.partial(share_kernel, n_rep),
        out_shape=[
            jax.ShapeDtypeStruct((4, n_rep * n, LANES), F32),
            jax.ShapeDtypeStruct((3, PART, tracts), F32),
        ],
        in_specs=[vmem] * 9,
        out_specs=[vmem] * 2,
        scratch_shapes=[
            pltpu.VMEM((4 * n, LANES), F32),
            pltpu.VMEM((n_rep, 4 * n, LANES), F32),
            pltpu.VMEM((3, n_rep * PART, tracts), F32),
            dma((n_rep - 1,)),
            dma((n_rep - 1,)),
        ],
        compiler_params=pltpu.CompilerParams(collective_id=0, has_side_effects=True),
        name="share",
    )(
        base.reshape(n, LANES),
        job_res.reshape(n, LANES),
        job_slot.reshape(n, LANES),
        job_cell.reshape(n, LANES),
        needed.reshape(1, LANES),
        lam_res,
        lam_work,
        target_res,
        target_work,
    )
    count = n_rep * n * LANES
    out = jax.ShapeDtypeStruct((cells, tracts), F32)
    *fast, flag = pl.pallas_call(
        functools.partial(newton_kernel, n_geo, n_rep),
        out_shape=[out] * 4 + [jax.ShapeDtypeStruct((8, LANES), F32)],
        in_specs=[vmem] * 2,
        out_specs=[vmem] * 5,
        scratch_shapes=[
            pltpu.VMEM((LANES, count), BF),
            pltpu.VMEM((LANES, count), F32),
            pltpu.VMEM((8, LANES), F32),
            pltpu.VMEM((6 * CAP, count), BF),
            pltpu.VMEM((6 * CAP, LANES), F32),
            pltpu.VMEM((CAP * LANES, tracts), BF),
            pltpu.VMEM((CAP * LANES, tracts), BF),
            pltpu.VMEM((4 * PART, CAP * LANES), BF),
            pltpu.VMEM((5, LANES, 1, LANES), F32),
            pltpu.VMEM((5, LANES, 1, LANES), F32),
            pltpu.VMEM((n_rep, 9 * PART, tracts), F32),
            dma((5,)),
            dma((5,)),
            dma((2, n_rep - 1)),
            dma((2, n_rep - 1)),
        ],
        compiler_params=pltpu.CompilerParams(
            collective_id=1, has_side_effects=True, vmem_limit_bytes=48 * 2**20
        ),
        name="newton",
    )(jobs, parts)
    return lax.cond(flag[0, 0] == 0.0, lambda: tuple(fast), lambda: tuple(general(*args)))


def solution(mesh):
    in_specs = (
        P(("geo", "rep")),
        P(("geo", "rep")),
        P(("geo", "rep")),
        P(("geo", "rep")),
        P("geo", None, None),
        P(None, "geo"),
        P(None, "geo"),
        P(None, "geo"),
        P(None, "geo"),
    )
    out_specs = (P(None, "geo"), P(None, "geo"), P(None, "geo"), P(None, "geo"))
    work = functools.partial(body, mesh.shape["geo"], mesh.shape["rep"])
    return jax.shard_map(work, mesh=mesh, in_specs=in_specs, out_specs=out_specs, check_vma=False)
```

```python
import functools

import jax
import jax.numpy as jnp
from jax import lax
from jax.experimental import pallas as pl
from jax.experimental.pallas import tpu as pltpu
from jax.sharding import PartitionSpec as P

BLK = 32
ITERS = 3
RIDGE = 0.5
MESH = pl.DeviceIdType.MESH
LANES = 128
PART = 8
SUB = 24
CAP = 48
STEEP = 128.0
FLAT = 1e-3
BF = jnp.bfloat16
F32 = jnp.float32


def gather(table, index, rows):
    high = index >> 7
    low = index & 127
    out = jnp.zeros(index.shape, F32)
    for row in range(rows):
        for half in range(2):
            line = table[row : row + 1, half * LANES : (half + 1) * LANES]
            line = jnp.broadcast_to(line, index.shape)
            out = jnp.where(high == 2 * row + half, jnp.take_along_axis(line, low, axis=1), out)
    return out


def split(x):
    high = x.astype(BF).astype(F32)
    return high, x - high


def newton_kernel(
    n_geo, n_rep, base, res, slot, cell, needed, lam_res, lam_work, t_res, t_work, o_all, o_flag,
    wide, ohp, pre, fields, place, xsend, xlist, oht_r, oht_w, left, send, recv, xbuf,
    list_send_sem, list_recv_sem, send_sem, recv_sem, xsend_sem, xrecv_sem,
):
    g, r = lax.axis_index("geo"), lax.axis_index("rep")
    barrier = pltpu.get_barrier_semaphore()

    depth = n_geo // 16
    z, y, core = g // 16, lax.rem(g // 2, 8), lax.rem(g, 2)
    lows = [
        lax.rem(y + d, 8) * 2 + lax.rem(core + e, 2)
        for d in (4, 3, 5, 2, 6, 1, 7, 0)
        for e in (1, 0)
    ]

    def each_peer(act):
        def plane(j, carry):
            high = lax.rem(z + j + 3, depth) * 16
            for low in lows[:-1]:
                act(high + low)
            return carry

        lax.fori_loop(0, depth, plane, 0)
        for d in range(1, depth):
            act(lax.rem(z + d, depth) * 16 + lows[-1])

    each_peer(
        lambda peer: pl.semaphore_signal(barrier, inc=1, device_id=(peer, r), device_id_type=MESH)
    )
    for i in range(1, n_rep):
        pl.semaphore_signal(
            barrier, inc=1, device_id=(g, lax.rem(r + i, n_rep)), device_id_type=MESH
        )

    cells = lam_res.shape[0]
    c = cell[...]
    s = slot[...]
    p = s >> 5
    block = jnp.take_along_axis(jnp.broadcast_to(needed[...], s.shape), p, axis=1)
    u_all = base[...] * jnp.exp(gather(lam_res[...], c * 256 + res[...], cells))
    bucket = (c >> 3) * LANES + p
    chunks = base.shape[0] // 2
    peers = lax.broadcasted_iota(jnp.int32, (n_rep * LANES, 2 * LANES), 0)

    def pair(x, k):
        return jnp.concatenate([x[2 * k : 2 * k + 1, :], x[2 * k + 1 : 2 * k + 2, :]], axis=1)

    before = lax.broadcasted_iota(jnp.int32, (2 * LANES, 2 * LANES), 0)
    after = lax.broadcasted_iota(jnp.int32, (2 * LANES, 2 * LANES), 1)
    upto = jnp.where(before <= after, 1.0, 0.0).astype(BF)
    for k in range(chunks):
        span = slice(k * 256, (k + 1) * 256)
        ohp[:, span] = jnp.where(pair(bucket, k) == peers, 1.0, 0.0).astype(BF)
    for k in range(chunks):
        span = slice(k * 256, (k + 1) * 256)
        pre[:, span] = jnp.dot(ohp[:, span], upto, preferred_element_type=F32)
    u_1 = u_all.astype(BF).astype(F32)
    u_2 = (u_all - u_1).astype(BF).astype(F32)
    kinds = (
        u_1,
        u_2,
        u_all - u_1 - u_2,
        (c & (PART - 1)).astype(F32),
        (block * BLK + (s & (BLK - 1))).astype(F32),
        res[...].astype(F32),
    )
    steps = lax.broadcasted_iota(jnp.int32, (SUB, 256), 0).astype(F32)
    so_far = jnp.zeros((n_rep * LANES, 1), F32)
    for k in range(chunks):
        span = slice(k * 256, (k + 1) * 256)
        here = pre[:, span]
        rank = jnp.sum(ohp[:, span].astype(F32) * (here + so_far), axis=0, keepdims=True) - 1.0
        so_far = so_far + here[:, 255:256]
        spot = rank == steps
        for f, kind in enumerate(kinds):
            fields[f * SUB : (f + 1) * SUB, span] = jnp.where(spot, pair(kind, k), 0.0).astype(BF)
    most = jnp.max(so_far)
    place[...] = lax.dot_general(
        fields[...], ohp[...], (((1,), (1,)), ((), ())), preferred_element_type=F32
    )
    for q in range(n_rep):
        lists = [
            place[f * SUB : (f + 1) * SUB, q * LANES : (q + 1) * LANES] for f in range(len(kinds))
        ]
        xsend[q, 0:SUB, :] = lists[0] + lists[1] + lists[2]
        xsend[q, SUB : 2 * SUB, :] = lists[3] * 256.0 + lists[4]
        xsend[q, 2 * SUB : 3 * SUB, :] = lists[3] * 256.0 + lists[5]
    for k, table in enumerate((lam_work, t_res, t_work)):
        wide[k] = jnp.zeros(wide.shape[1:], F32)
        wide[k, 0:cells, :] = table[...]
    mine = pl.ds(pl.multiple_of(r * PART, PART), PART)
    parts = [wide[k, mine, :] for k in range(3)]
    pl.semaphore_wait(barrier, n_geo - 1 + n_rep - 1)

    copies = []
    for i in range(1, n_rep):
        other = lax.rem(r + i, n_rep)
        copy = pltpu.make_async_remote_copy(
            src_ref=xsend.at[other],
            dst_ref=xlist.at[r],
            send_sem=list_send_sem.at[i - 1],
            recv_sem=list_recv_sem.at[i - 1],
            device_id=(g, other),
            device_id_type=MESH,
        )
        copy.start()
        copies.append(copy)
    xlist[r] = xsend[r]
    for copy in copies:
        copy.wait()
    merged = [jnp.zeros((CAP, LANES), F32)] * 3
    offset = jnp.zeros((1, LANES), jnp.int32)
    empty = jnp.zeros((CAP - SUB, LANES), F32)
    for q in range(n_rep):
        lists = [xlist[q, f * SUB : (f + 1) * SUB, :] for f in range(3)]
        count = jnp.sum(jnp.where(lists[0] > 0.0, 1, 0), axis=0, keepdims=True)
        lists = [jnp.concatenate([x, empty], axis=0) for x in lists]
        if q:
            for bit in range(6):
                moved = (offset >> bit) & 1 == 1
                width = 1 << bit
                gap = jnp.zeros((width, LANES), F32)
                lists = [
                    jnp.where(moved, jnp.concatenate([gap, x[: CAP - width]], axis=0), x)
                    for x in lists
                ]
        merged = [x + y for x, y in zip(merged, lists)]
        offset = offset + count
    crowded = jnp.logical_or(most > SUB, jnp.max(offset) > CAP)
    u_g, work_g, home_g = merged
    home_g = home_g.astype(jnp.int32)
    cell_g = home_g >> 8
    res_g = (home_g & 255).astype(F32)

    pad = jnp.zeros((LANES - 2 * CAP, LANES), F32)

    def launch(k, first, second):
        whole = jnp.concatenate([first, second, pad], axis=0)
        send[k] = jnp.transpose(whole).reshape(LANES, 1, LANES)

        each_peer(
            lambda peer: pltpu.make_async_remote_copy(
                src_ref=send.at[k, peer],
                dst_ref=recv.at[k, g],
                send_sem=send_sem.at[k],
                recv_sem=recv_sem.at[k],
                device_id=(peer, r),
                device_id_type=MESH,
            ).start()
        )
        recv[k, g] = send[k, g]

    def everything(k):
        return pltpu.make_async_remote_copy(
            src_ref=send.at[k, pl.ds(0, n_geo - 1)],
            dst_ref=recv.at[k, pl.ds(0, n_geo - 1)],
            send_sem=send_sem.at[k],
            recv_sem=recv_sem.at[k],
            device_id=(g, r),
            device_id_type=MESH,
        )

    def arrive(k):
        everything(k).wait_recv()
        return jnp.transpose(recv[k].reshape(LANES, LANES))

    def over(x):
        x = x.astype(F32)
        return jnp.transpose(jnp.concatenate([x, jnp.zeros((LANES - CAP, LANES), F32)], axis=0))

    tracts = lax.broadcasted_iota(jnp.int32, (LANES, 256), 1).astype(F32)

    def columns(oht, numbers):
        for k in range(CAP):
            hot = jnp.where(numbers[:, k : k + 1] == tracts, 1.0, 0.0)
            oht[k * LANES : (k + 1) * LANES, :] = hot.astype(BF)

    lines = lax.broadcasted_iota(jnp.int32, (PART, LANES), 0)

    def scatter(values, cell, oht):
        pieces = [piece for value in values for piece in split(value)]
        for k in range(CAP):
            mine = cell[k : k + 1, :] == lines
            stack = [jnp.where(mine, piece[k : k + 1, :], 0.0) for piece in pieces]
            left[0 : PART * len(pieces), k * LANES : (k + 1) * LANES] = jnp.concatenate(
                stack, axis=0
            ).astype(BF)
        out = jnp.dot(left[0 : PART * len(pieces), :], oht[...], preferred_element_type=F32)
        return [
            out[2 * v * PART : (2 * v + 1) * PART] + out[(2 * v + 1) * PART : (2 * v + 2) * PART]
            for v in range(len(values))
        ]

    launch(0, u_g, work_g)
    columns(oht_r, over(res_g))

    flat = arrive(0)
    u_o = flat[0:CAP]
    work_o = flat[CAP : 2 * CAP].astype(jnp.int32)
    cell_o = work_o >> 8
    columns(oht_w, over(work_o & 255))
    w_o = u_o * gather(jnp.exp(parts[0]), work_o, PART)
    [sum_w] = scatter([w_o], cell_o, oht_w)
    diag_w = sum_w + RIDGE
    b0 = parts[2] - sum_w
    launch(1, w_o, gather(b0, work_o, PART))

    flat = arrive(1)
    w_g = flat[0:CAP]
    sum_r, bb0 = scatter([w_g, w_g * flat[CAP : 2 * CAP]], cell_g, oht_r)
    diag_r = sum_r + RIDGE
    a0 = parts[1] - sum_r
    a1 = diag_r * a0 + bb0
    launch(2, w_g * gather(a0, home_g, PART), w_g * gather(a1, home_g, PART))

    flat = arrive(2)
    ba0, ba1 = scatter([flat[0:CAP], flat[CAP : 2 * CAP]], cell_o, oht_w)
    b1 = diag_w * b0 + ba0
    b2 = diag_w * b1 + ba1
    launch(3, w_o * gather(b1, work_o, PART), w_o * gather(b2, work_o, PART))

    flat = arrive(3)
    bb1, bb2 = scatter([flat[0:CAP], flat[CAP : 2 * CAP]], cell_g, oht_r)
    a2 = diag_r * a1 + bb1
    a3 = diag_r * a2 + bb2

    def line(x):
        x = x[:, 0:LANES] + x[:, LANES : 2 * LANES]
        return jnp.sum(x, axis=0, keepdims=True)

    steep = jnp.maximum(jnp.max(sum_r), jnp.max(sum_w))
    bad = jnp.where(jnp.logical_or(steep > STEEP, crowded), 1.0, 0.0)
    table = jnp.concatenate(
        [
            line(a0 * a0 + b0 * b0),
            line(a0 * a1 + b0 * b1),
            line(a1 * a1 + b1 * b1),
            line(a1 * a2 + b1 * b2),
            line(a2 * a2 + b2 * b2),
            line(a2 * (a3 + bb2) + diag_w * b2 * b2),
            jnp.full((1, LANES), bad, F32),
            jnp.zeros((1, LANES), F32),
        ],
        axis=0,
    )
    table = jnp.broadcast_to(jnp.sum(table, axis=1, keepdims=True), (8, LANES))
    launch(
        4,
        w_g * gather(a2, home_g, PART),
        jnp.concatenate([table, jnp.zeros((CAP - 8, LANES), F32)], axis=0),
    )

    early = 7 * PART
    for v, vector in enumerate((a0, a1, a2, a3, b0, b1, b2)):
        xbuf[r, v * PART : (v + 1) * PART, :] = vector

    def across(lo, hi, which):
        copies = []
        for i in range(1, n_rep):
            copy = pltpu.make_async_remote_copy(
                src_ref=xbuf.at[r, pl.ds(lo, hi - lo)],
                dst_ref=xbuf.at[r, pl.ds(lo, hi - lo)],
                send_sem=xsend_sem.at[which, i - 1],
                recv_sem=xrecv_sem.at[which, i - 1],
                device_id=(g, lax.rem(r + i, n_rep)),
                device_id_type=MESH,
            )
            copy.start()
            copies.append(copy)
        return copies

    first = across(0, early, 0)

    flat = arrive(4)
    [ba2] = scatter([flat[0:CAP]], cell_o, oht_w)
    b3 = diag_w * b2 + ba2
    xbuf[r, early : early + PART, :] = b3
    xbuf[r, early + PART : early + 2 * PART, :] = jnp.broadcast_to(
        jnp.sum(flat[CAP : CAP + 8], axis=1, keepdims=True), (8, 256)
    )
    last = across(early, early + 2 * PART, 1)
    for copy in first + last:
        copy.wait()
    for k in range(5):
        everything(k).wait_send()

    sums = xbuf[0, early + PART : early + 2 * PART, :]
    for q in range(1, n_rep):
        sums = sums + xbuf[q, early + PART : early + 2 * PART, :]
    m = [sums[i : i + 1, :] for i in range(7)]

    def form(x, shift):
        n = len(x)
        total = None
        for s in range(2 * n - 1):
            part = None
            for i in range(max(0, s - n + 1), min(n - 1, s) + 1):
                term = x[i] * x[s - i]
                part = term if part is None else part + term
            part = part * m[s + shift]
            total = part if total is None else total + part
        return total

    one = jnp.ones((1, 256), F32)
    rc, pc, xc = [one], [one], []
    norm = m[0]
    for turn in range(ITERS):
        alpha = norm / form(pc, 1)
        xc = [x + alpha * p for x, p in zip(xc, pc)] + [alpha * pc[-1]]
        image = [-alpha * p for p in pc]
        rc = [rc[0]] + [x + y for x, y in zip(rc[1:], image[:-1])] + [image[-1]]
        if turn < ITERS - 1:
            new = form(rc, 0)
            beta = new / norm
            pc = [x + beta * p for x, p in zip(rc[:-1], pc)] + [rc[-1]]
            norm = new
    good = jnp.logical_and(m[6] == 0.0, norm > FLAT * m[0])
    o_flag[0, 0] = jnp.max(jnp.where(good, 0, 1))
    for q in range(n_rep):
        lo = q * PART
        for side in range(2):
            k = [xbuf[q, (4 * side + i) * PART : (4 * side + i + 1) * PART, :] for i in range(4)]
            o_all[side, lo : lo + PART, :] = xc[0] * k[0] + xc[1] * k[1] + xc[2] * k[2]
            o_all[2 + side, lo : lo + PART, :] = k[0] + rc[1] * k[1] + rc[2] * k[2] + rc[3] * k[3]


def hand_out(stack, *outs):
    for k, out in enumerate(outs):
        out[...] = stack[k, 0 : out.shape[0], :]


def general(base, job_res, job_slot, job_cell, needed, lam_res, lam_work, target_res, target_work):
    cells, tracts_dev = lam_res.shape
    blocks_dev = tracts_dev // BLK
    requests = lax.all_to_all(needed[0], "geo", split_axis=0, concat_axis=0, tiled=True)
    sources, listed = requests.shape
    hot = requests[:, :, None] == jnp.arange(blocks_dev, dtype=jnp.int32)[None, None, :]
    onehot = hot.astype(jnp.float32)
    slot_shape = (sources, listed, cells, BLK)
    slot_count = sources * listed * cells * BLK
    res_index = job_cell * tracts_dev + job_res
    work_index = (job_slot // BLK * cells + job_cell) * BLK + job_slot % BLK

    def serve(table):
        blocks = table.reshape(cells, blocks_dev, BLK).transpose(1, 0, 2)
        out = jnp.zeros(slot_shape, jnp.float32)
        for b in range(blocks_dev):
            out = jnp.where(hot[:, :, b, None, None], blocks[b][None, None], out)
        return out

    def pick(fetched):
        return fetched.reshape(-1)[work_index]

    def fold(arrived):
        return jnp.einsum("skb,skcx->cbx", onehot, arrived, precision=lax.Precision.HIGHEST)

    def totals(values):
        res_part = jax.ops.segment_sum(values, res_index, num_segments=cells * tracts_dev).reshape(
            cells, tracts_dev
        )
        work_part = jax.ops.segment_sum(values, work_index, num_segments=slot_count).reshape(
            slot_shape
        )
        arrived = lax.all_to_all(work_part, "geo", split_axis=0, concat_axis=0, tiled=True)
        folded = fold(arrived)
        return lax.psum((res_part, folded.reshape(cells, tracts_dev)), "rep")

    def squares(part_res, part_work):
        local = jnp.sum(part_res * part_res) + jnp.sum(part_work * part_work)
        return lax.psum(local, "geo")

    def fetch(table):
        return lax.all_to_all(serve(table), "geo", split_axis=0, concat_axis=0, tiled=True)

    weight = base * jnp.exp(lam_res.reshape(-1)[res_index] + pick(fetch(lam_work)))
    total_res, total_work = totals(weight)
    resid_res = -(total_res - target_res)
    resid_work = -(total_work - target_work)
    zero = jnp.zeros_like(resid_res)
    norm = squares(resid_res, resid_work)

    def turn(_, state):
        step_res, step_work, resid_res, resid_work, dir_res, dir_work, norm_now = state
        along = dir_res.reshape(-1)[res_index] + pick(fetch(dir_work))
        image_res, image_work = totals(weight * along)
        image_res = image_res + RIDGE * dir_res
        image_work = image_work + RIDGE * dir_work
        local_curv = jnp.sum(dir_res * image_res) + jnp.sum(dir_work * image_work)
        alpha = norm_now / lax.psum(local_curv, "geo")
        step_res = step_res + alpha * dir_res
        step_work = step_work + alpha * dir_work
        resid_res = resid_res - alpha * image_res
        resid_work = resid_work - alpha * image_work
        norm_next = squares(resid_res, resid_work)
        dir_res = resid_res + norm_next / norm_now * dir_res
        dir_work = resid_work + norm_next / norm_now * dir_work
        return step_res, step_work, resid_res, resid_work, dir_res, dir_work, norm_next

    state = (zero, zero, resid_res, resid_work, resid_res, resid_work, norm)
    return lax.fori_loop(0, ITERS, turn, state)[:4]


def body(n_geo, n_rep, *args):
    base, job_res, job_slot, job_cell, needed, lam_res, lam_work, target_res, target_work = args
    n = base.shape[0] // LANES
    cells, tracts = lam_res.shape
    vmem = pl.BlockSpec(memory_space=pltpu.VMEM)
    dma = pltpu.SemaphoreType.DMA
    smem = pl.BlockSpec(memory_space=pltpu.SMEM)
    jobs = n * LANES
    stack, flag = pl.pallas_call(
        functools.partial(newton_kernel, n_geo, n_rep),
        out_shape=[
            jax.ShapeDtypeStruct((4, n_rep * PART, tracts), F32),
            jax.ShapeDtypeStruct((1, 1), jnp.int32),
        ],
        in_specs=[vmem] * 9,
        out_specs=[vmem, smem],
        scratch_shapes=[
            pltpu.VMEM((3, n_rep * PART, tracts), F32),
            pltpu.VMEM((n_rep * LANES, jobs), BF),
            pltpu.VMEM((n_rep * LANES, jobs), F32),
            pltpu.VMEM((6 * SUB, jobs), BF),
            pltpu.VMEM((6 * SUB, n_rep * LANES), F32),
            pltpu.VMEM((n_rep, 3 * SUB, LANES), F32),
            pltpu.VMEM((n_rep, 3 * SUB, LANES), F32),
            pltpu.VMEM((CAP * LANES, tracts), BF),
            pltpu.VMEM((CAP * LANES, tracts), BF),
            pltpu.VMEM((4 * PART, CAP * LANES), BF),
            pltpu.VMEM((5, LANES, 1, LANES), F32),
            pltpu.VMEM((5, LANES, 1, LANES), F32),
            pltpu.VMEM((n_rep, 9 * PART, tracts), F32),
            dma((n_rep - 1,)),
            dma((n_rep - 1,)),
            dma((5,)),
            dma((5,)),
            dma((2, n_rep - 1)),
            dma((2, n_rep - 1)),
        ],
        compiler_params=pltpu.CompilerParams(
            collective_id=0, has_side_effects=True, vmem_limit_bytes=40 * 2**20
        ),
        name="newton",
    )(
        base.reshape(n, LANES),
        job_res.reshape(n, LANES),
        job_slot.reshape(n, LANES),
        job_cell.reshape(n, LANES),
        needed.reshape(1, LANES),
        lam_res,
        lam_work,
        target_res,
        target_work,
    )
    out = jax.ShapeDtypeStruct((cells, tracts), F32)

    def fast():
        return tuple(
            pl.pallas_call(
                hand_out, out_shape=[out] * 4, in_specs=[vmem], out_specs=[vmem] * 4, name="finish"
            )(stack)
        )

    return lax.cond(flag[0, 0] == 0, fast, lambda: tuple(general(*args)))


def solution(mesh):
    in_specs = (
        P(("geo", "rep")),
        P(("geo", "rep")),
        P(("geo", "rep")),
        P(("geo", "rep")),
        P("geo", None, None),
        P(None, "geo"),
        P(None, "geo"),
        P(None, "geo"),
        P(None, "geo"),
    )
    out_specs = (P(None, "geo"), P(None, "geo"), P(None, "geo"), P(None, "geo"))
    work = functools.partial(body, mesh.shape["geo"], mesh.shape["rep"])
    return jax.shard_map(work, mesh=mesh, in_specs=in_specs, out_specs=out_specs, check_vma=False)
```

```python
import functools

import jax
import jax.numpy as jnp
from jax import lax
from jax.experimental import pallas as pl
from jax.experimental.pallas import tpu as pltpu
from jax.sharding import PartitionSpec as P

BLK = 32
ITERS = 3
RIDGE = 0.5
MESH = pl.DeviceIdType.MESH
LANES = 128
PART = 8
SUB = 24
CAP = 48
STEEP = 128.0
FLAT = 1e-3
BF = jnp.bfloat16
F32 = jnp.float32


def gather(table, index, rows):
    high = index >> 7
    low = index & 127
    out = jnp.zeros(index.shape, F32)
    for row in range(rows):
        for half in range(2):
            line = table[row : row + 1, half * LANES : (half + 1) * LANES]
            line = jnp.broadcast_to(line, index.shape)
            out = jnp.where(high == 2 * row + half, jnp.take_along_axis(line, low, axis=1), out)
    return out


def split(x):
    high = x.astype(BF).astype(F32)
    return high, x - high


def newton_kernel(
    n_geo, n_rep, base, res, slot, cell, needed, lam_res, lam_work, t_res, t_work, o_all, o_flag,
    wide, ohp, pre, fields, place, xsend, xlist, oht_r, oht_w, left, send, recv, xbuf,
    list_send_sem, list_recv_sem, send_sem, recv_sem, xsend_sem, xrecv_sem,
):
    g, r = lax.axis_index("geo"), lax.axis_index("rep")
    barrier = pltpu.get_barrier_semaphore()

    depth = n_geo // 16
    z, y, core = g // 16, lax.rem(g // 2, 8), lax.rem(g, 2)
    lows = [
        lax.rem(y + d, 8) * 2 + lax.rem(core + e, 2)
        for d in (4, 3, 5, 2, 6, 1, 7, 0)
        for e in (1, 0)
    ]

    def each_peer(act):
        def plane(j, carry):
            high = lax.rem(z + j + 3, depth) * 16
            for low in lows[:-1]:
                act(high + low)
            return carry

        lax.fori_loop(0, depth, plane, 0)
        for d in range(1, depth):
            act(lax.rem(z + d, depth) * 16 + lows[-1])

    each_peer(
        lambda peer: pl.semaphore_signal(barrier, inc=1, device_id=(peer, r), device_id_type=MESH)
    )
    for i in range(1, n_rep):
        pl.semaphore_signal(
            barrier, inc=1, device_id=(g, lax.rem(r + i, n_rep)), device_id_type=MESH
        )

    cells = lam_res.shape[0]
    c = cell[...]
    s = slot[...]
    p = s >> 5
    block = jnp.take_along_axis(jnp.broadcast_to(needed[...], s.shape), p, axis=1)
    u_all = base[...] * jnp.exp(gather(lam_res[...], c * 256 + res[...], cells))
    bucket = (c >> 3) * LANES + p
    chunks = base.shape[0] // 2
    peers = lax.broadcasted_iota(jnp.int32, (n_rep * LANES, 2 * LANES), 0)

    def pair(x, k):
        return jnp.concatenate([x[2 * k : 2 * k + 1, :], x[2 * k + 1 : 2 * k + 2, :]], axis=1)

    before = lax.broadcasted_iota(jnp.int32, (2 * LANES, 2 * LANES), 0)
    after = lax.broadcasted_iota(jnp.int32, (2 * LANES, 2 * LANES), 1)
    upto = jnp.where(before <= after, 1.0, 0.0).astype(BF)
    for k in range(chunks):
        span = slice(k * 256, (k + 1) * 256)
        ohp[:, span] = jnp.where(pair(bucket, k) == peers, 1.0, 0.0).astype(BF)
    for k in range(chunks):
        span = slice(k * 256, (k + 1) * 256)
        pre[:, span] = jnp.dot(ohp[:, span], upto, preferred_element_type=F32)
    u_1 = u_all.astype(BF).astype(F32)
    u_2 = (u_all - u_1).astype(BF).astype(F32)
    kinds = (
        u_1,
        u_2,
        u_all - u_1 - u_2,
        (c & (PART - 1)).astype(F32),
        (block * BLK + (s & (BLK - 1))).astype(F32),
        res[...].astype(F32),
    )
    steps = lax.broadcasted_iota(jnp.int32, (SUB, 256), 0).astype(F32)
    so_far = jnp.zeros((n_rep * LANES, 1), F32)
    for k in range(chunks):
        span = slice(k * 256, (k + 1) * 256)
        here = pre[:, span]
        rank = jnp.sum(ohp[:, span].astype(F32) * (here + so_far), axis=0, keepdims=True) - 1.0
        so_far = so_far + here[:, 255:256]
        spot = rank == steps
        for f, kind in enumerate(kinds):
            fields[f * SUB : (f + 1) * SUB, span] = jnp.where(spot, pair(kind, k), 0.0).astype(BF)
    most = jnp.max(so_far)
    place[...] = lax.dot_general(
        fields[...], ohp[...], (((1,), (1,)), ((), ())), preferred_element_type=F32
    )
    for q in range(n_rep):
        lists = [
            place[f * SUB : (f + 1) * SUB, q * LANES : (q + 1) * LANES] for f in range(len(kinds))
        ]
        xsend[q, 0:SUB, :] = lists[0] + lists[1] + lists[2]
        xsend[q, SUB : 2 * SUB, :] = lists[3] * 256.0 + lists[4]
        xsend[q, 2 * SUB : 3 * SUB, :] = lists[3] * 256.0 + lists[5]
    for k, table in enumerate((lam_work, t_res, t_work)):
        wide[k] = jnp.zeros(wide.shape[1:], F32)
        wide[k, 0:cells, :] = table[...]
    mine = pl.ds(pl.multiple_of(r * PART, PART), PART)
    parts = [wide[k, mine, :] for k in range(3)]
    pl.semaphore_wait(barrier, n_geo - 1 + n_rep - 1)

    def swap(lo, hi, which):
        copies = []
        for i in range(1, n_rep):
            other = lax.rem(r + i, n_rep)
            copy = pltpu.make_async_remote_copy(
                src_ref=xsend.at[other, pl.ds(lo, hi - lo)],
                dst_ref=xlist.at[r, pl.ds(lo, hi - lo)],
                send_sem=list_send_sem.at[which, i - 1],
                recv_sem=list_recv_sem.at[which, i - 1],
                device_id=(g, other),
                device_id_type=MESH,
            )
            copy.start()
            copies.append(copy)
        return copies

    lists_now = swap(0, 2 * SUB, 0)
    lists_later = swap(2 * SUB, 3 * SUB, 1)
    xlist[r] = xsend[r]
    for copy in lists_now:
        copy.wait()

    counts = [
        jnp.sum(jnp.where(xlist[q, 0:SUB, :] > 0.0, 1, 0), axis=0, keepdims=True)
        for q in range(n_rep)
    ]

    def merge(field):
        total = jnp.zeros((CAP, LANES), F32)
        offset = jnp.zeros((1, LANES), jnp.int32)
        for q in range(n_rep):
            x = xlist[q, field * SUB : (field + 1) * SUB, :]
            x = jnp.concatenate([x, jnp.zeros((CAP - SUB, LANES), F32)], axis=0)
            if q:
                for bit in range(6):
                    width = 1 << bit
                    gap = jnp.zeros((width, LANES), F32)
                    down = jnp.concatenate([gap, x[: CAP - width]], axis=0)
                    x = jnp.where((offset >> bit) & 1 == 1, down, x)
            total = total + x
            offset = offset + counts[q]
        return total

    crowded = jnp.logical_or(
        most > SUB, jnp.max(counts[0] + counts[1] + counts[2] + counts[3]) > CAP
    )

    pad = jnp.zeros((LANES - 2 * CAP, LANES), F32)

    def launch(k, first, second):
        whole = jnp.concatenate([first, second, pad], axis=0)
        send[k] = jnp.transpose(whole)

        each_peer(
            lambda peer: pltpu.make_async_remote_copy(
                src_ref=send.at[k, pl.ds(peer, 1)],
                dst_ref=recv.at[k, pl.ds(g, 1)],
                send_sem=send_sem.at[k],
                recv_sem=recv_sem.at[k],
                device_id=(peer, r),
                device_id_type=MESH,
            ).start()
        )
        recv[k, pl.ds(g, 1), :] = send[k, pl.ds(g, 1), :]

    def everything(k):
        return pltpu.make_async_remote_copy(
            src_ref=send.at[k, pl.ds(0, n_geo - 1)],
            dst_ref=recv.at[k, pl.ds(0, n_geo - 1)],
            send_sem=send_sem.at[k],
            recv_sem=recv_sem.at[k],
            device_id=(g, r),
            device_id_type=MESH,
        )

    def arrive(k):
        everything(k).wait_recv()
        return jnp.transpose(recv[k])

    def over(x):
        x = x.astype(F32)
        return jnp.transpose(jnp.concatenate([x, jnp.zeros((LANES - CAP, LANES), F32)], axis=0))

    tracts = lax.broadcasted_iota(jnp.int32, (LANES, LANES), 1).astype(F32)

    def columns(oht, numbers):
        for k in range(CAP):
            hot = jnp.where(numbers[:, k : k + 1] == tracts, 1.0, 0.0)
            oht[k * LANES : (k + 1) * LANES, :] = hot.astype(BF)

    lines = lax.broadcasted_iota(jnp.int32, (2 * PART, LANES), 0)

    def line_of(index):
        return (index >> 8) + PART * ((index >> 7) & 1)

    def scatter(values, line, oht):
        pieces = [piece for value in values for piece in split(value)]
        high = 2 * PART
        for k in range(CAP):
            mine = line[k : k + 1, :] == lines
            stack = [jnp.where(mine, piece[k : k + 1, :], 0.0) for piece in pieces]
            left[0 : high * len(pieces), k * LANES : (k + 1) * LANES] = jnp.concatenate(
                stack, axis=0
            ).astype(BF)
        out = jnp.dot(left[0 : high * len(pieces), :], oht[...], preferred_element_type=F32)
        sums = [
            out[2 * v * high : (2 * v + 1) * high] + out[(2 * v + 1) * high : (2 * v + 2) * high]
            for v in range(len(values))
        ]
        return [jnp.concatenate([x[:PART], x[PART:]], axis=1) for x in sums]

    launch(0, merge(0), merge(1))
    for copy in lists_later:
        copy.wait()
    home_g = merge(2).astype(jnp.int32)
    line_g = line_of(home_g)
    columns(oht_r, over(home_g & 127))

    flat = arrive(0)
    u_o = flat[0:CAP]
    work_o = flat[CAP : 2 * CAP].astype(jnp.int32)
    line_o = line_of(work_o)
    columns(oht_w, over(work_o & 127))
    w_o = u_o * gather(jnp.exp(parts[0]), work_o, PART)
    [sum_w] = scatter([w_o], line_o, oht_w)
    diag_w = sum_w + RIDGE
    b0 = parts[2] - sum_w
    launch(1, w_o, gather(b0, work_o, PART))

    flat = arrive(1)
    w_g = flat[0:CAP]
    sum_r, bb0 = scatter([w_g, w_g * flat[CAP : 2 * CAP]], line_g, oht_r)
    diag_r = sum_r + RIDGE
    a0 = parts[1] - sum_r
    a1 = diag_r * a0 + bb0
    launch(2, w_g * gather(a0, home_g, PART), w_g * gather(a1, home_g, PART))

    flat = arrive(2)
    ba0, ba1 = scatter([flat[0:CAP], flat[CAP : 2 * CAP]], line_o, oht_w)
    b1 = diag_w * b0 + ba0
    b2 = diag_w * b1 + ba1
    launch(3, w_o * gather(b1, work_o, PART), w_o * gather(b2, work_o, PART))

    flat = arrive(3)
    bb1, bb2 = scatter([flat[0:CAP], flat[CAP : 2 * CAP]], line_g, oht_r)
    a2 = diag_r * a1 + bb1
    a3 = diag_r * a2 + bb2

    def line(x):
        x = x[:, 0:LANES] + x[:, LANES : 2 * LANES]
        return jnp.sum(x, axis=0, keepdims=True)

    steep = jnp.maximum(jnp.max(sum_r), jnp.max(sum_w))
    bad = jnp.where(jnp.logical_or(steep > STEEP, crowded), 1.0, 0.0)
    table = jnp.concatenate(
        [
            line(a0 * a0 + b0 * b0),
            line(a0 * a1 + b0 * b1),
            line(a1 * a1 + b1 * b1),
            line(a1 * a2 + b1 * b2),
            line(a2 * a2 + b2 * b2),
            line(a2 * (a3 + bb2) + diag_w * b2 * b2),
            jnp.full((1, LANES), bad, F32),
            jnp.zeros((1, LANES), F32),
        ],
        axis=0,
    )
    table = jnp.broadcast_to(jnp.sum(table, axis=1, keepdims=True), (8, LANES))
    launch(
        4,
        w_g * gather(a2, home_g, PART),
        jnp.concatenate([table, jnp.zeros((CAP - 8, LANES), F32)], axis=0),
    )

    early = 7 * PART
    for v, vector in enumerate((a0, a1, a2, a3, b0, b1, b2)):
        xbuf[r, v * PART : (v + 1) * PART, :] = vector

    def across(lo, hi, which):
        copies = []
        for i in range(1, n_rep):
            copy = pltpu.make_async_remote_copy(
                src_ref=xbuf.at[r, pl.ds(lo, hi - lo)],
                dst_ref=xbuf.at[r, pl.ds(lo, hi - lo)],
                send_sem=xsend_sem.at[which, i - 1],
                recv_sem=xrecv_sem.at[which, i - 1],
                device_id=(g, lax.rem(r + i, n_rep)),
                device_id_type=MESH,
            )
            copy.start()
            copies.append(copy)
        return copies

    first = across(0, early, 0)

    flat = arrive(4)
    [ba2] = scatter([flat[0:CAP]], line_o, oht_w)
    b3 = diag_w * b2 + ba2
    xbuf[r, early : early + PART, :] = b3
    xbuf[r, early + PART : early + 2 * PART, :] = jnp.broadcast_to(
        jnp.sum(flat[CAP : CAP + 8], axis=1, keepdims=True), (8, 256)
    )
    last = across(early, early + 2 * PART, 1)
    for copy in first + last:
        copy.wait()
    for k in range(5):
        everything(k).wait_send()

    sums = xbuf[0, early + PART : early + 2 * PART, :]
    for q in range(1, n_rep):
        sums = sums + xbuf[q, early + PART : early + 2 * PART, :]
    m = [sums[i : i + 1, :] for i in range(7)]

    def form(x, shift):
        n = len(x)
        total = None
        for s in range(2 * n - 1):
            part = None
            for i in range(max(0, s - n + 1), min(n - 1, s) + 1):
                term = x[i] * x[s - i]
                part = term if part is None else part + term
            part = part * m[s + shift]
            total = part if total is None else total + part
        return total

    one = jnp.ones((1, 256), F32)
    rc, pc, xc = [one], [one], []
    norm = m[0]
    for turn in range(ITERS):
        alpha = norm / form(pc, 1)
        xc = [x + alpha * p for x, p in zip(xc, pc)] + [alpha * pc[-1]]
        image = [-alpha * p for p in pc]
        rc = [rc[0]] + [x + y for x, y in zip(rc[1:], image[:-1])] + [image[-1]]
        if turn < ITERS - 1:
            new = form(rc, 0)
            beta = new / norm
            pc = [x + beta * p for x, p in zip(rc[:-1], pc)] + [rc[-1]]
            norm = new
    good = jnp.logical_and(m[6] == 0.0, norm > FLAT * m[0])
    o_flag[0, 0] = jnp.max(jnp.where(good, 0, 1))
    for q in range(n_rep):
        lo = q * PART
        for side in range(2):
            k = [xbuf[q, (4 * side + i) * PART : (4 * side + i + 1) * PART, :] for i in range(4)]
            o_all[side, lo : lo + PART, :] = xc[0] * k[0] + xc[1] * k[1] + xc[2] * k[2]
            o_all[2 + side, lo : lo + PART, :] = k[0] + rc[1] * k[1] + rc[2] * k[2] + rc[3] * k[3]


def hand_out(stack, *outs):
    for k, out in enumerate(outs):
        out[...] = stack[k, 0 : out.shape[0], :]


def general(base, job_res, job_slot, job_cell, needed, lam_res, lam_work, target_res, target_work):
    cells, tracts_dev = lam_res.shape
    blocks_dev = tracts_dev // BLK
    requests = lax.all_to_all(needed[0], "geo", split_axis=0, concat_axis=0, tiled=True)
    sources, listed = requests.shape
    hot = requests[:, :, None] == jnp.arange(blocks_dev, dtype=jnp.int32)[None, None, :]
    onehot = hot.astype(jnp.float32)
    slot_shape = (sources, listed, cells, BLK)
    slot_count = sources * listed * cells * BLK
    res_index = job_cell * tracts_dev + job_res
    work_index = (job_slot // BLK * cells + job_cell) * BLK + job_slot % BLK

    def serve(table):
        blocks = table.reshape(cells, blocks_dev, BLK).transpose(1, 0, 2)
        out = jnp.zeros(slot_shape, jnp.float32)
        for b in range(blocks_dev):
            out = jnp.where(hot[:, :, b, None, None], blocks[b][None, None], out)
        return out

    def pick(fetched):
        return fetched.reshape(-1)[work_index]

    def fold(arrived):
        return jnp.einsum("skb,skcx->cbx", onehot, arrived, precision=lax.Precision.HIGHEST)

    def totals(values):
        res_part = jax.ops.segment_sum(values, res_index, num_segments=cells * tracts_dev).reshape(
            cells, tracts_dev
        )
        work_part = jax.ops.segment_sum(values, work_index, num_segments=slot_count).reshape(
            slot_shape
        )
        arrived = lax.all_to_all(work_part, "geo", split_axis=0, concat_axis=0, tiled=True)
        folded = fold(arrived)
        return lax.psum((res_part, folded.reshape(cells, tracts_dev)), "rep")

    def squares(part_res, part_work):
        local = jnp.sum(part_res * part_res) + jnp.sum(part_work * part_work)
        return lax.psum(local, "geo")

    def fetch(table):
        return lax.all_to_all(serve(table), "geo", split_axis=0, concat_axis=0, tiled=True)

    weight = base * jnp.exp(lam_res.reshape(-1)[res_index] + pick(fetch(lam_work)))
    total_res, total_work = totals(weight)
    resid_res = -(total_res - target_res)
    resid_work = -(total_work - target_work)
    zero = jnp.zeros_like(resid_res)
    norm = squares(resid_res, resid_work)

    def turn(_, state):
        step_res, step_work, resid_res, resid_work, dir_res, dir_work, norm_now = state
        along = dir_res.reshape(-1)[res_index] + pick(fetch(dir_work))
        image_res, image_work = totals(weight * along)
        image_res = image_res + RIDGE * dir_res
        image_work = image_work + RIDGE * dir_work
        local_curv = jnp.sum(dir_res * image_res) + jnp.sum(dir_work * image_work)
        alpha = norm_now / lax.psum(local_curv, "geo")
        step_res = step_res + alpha * dir_res
        step_work = step_work + alpha * dir_work
        resid_res = resid_res - alpha * image_res
        resid_work = resid_work - alpha * image_work
        norm_next = squares(resid_res, resid_work)
        dir_res = resid_res + norm_next / norm_now * dir_res
        dir_work = resid_work + norm_next / norm_now * dir_work
        return step_res, step_work, resid_res, resid_work, dir_res, dir_work, norm_next

    state = (zero, zero, resid_res, resid_work, resid_res, resid_work, norm)
    return lax.fori_loop(0, ITERS, turn, state)[:4]


def body(n_geo, n_rep, *args):
    base, job_res, job_slot, job_cell, needed, lam_res, lam_work, target_res, target_work = args
    n = base.shape[0] // LANES
    cells, tracts = lam_res.shape
    vmem = pl.BlockSpec(memory_space=pltpu.VMEM)
    dma = pltpu.SemaphoreType.DMA
    smem = pl.BlockSpec(memory_space=pltpu.SMEM)
    jobs = n * LANES
    stack, flag = pl.pallas_call(
        functools.partial(newton_kernel, n_geo, n_rep),
        out_shape=[
            jax.ShapeDtypeStruct((4, n_rep * PART, tracts), F32),
            jax.ShapeDtypeStruct((1, 1), jnp.int32),
        ],
        in_specs=[vmem] * 9,
        out_specs=[vmem, smem],
        scratch_shapes=[
            pltpu.VMEM((3, n_rep * PART, tracts), F32),
            pltpu.VMEM((n_rep * LANES, jobs), BF),
            pltpu.VMEM((n_rep * LANES, jobs), F32),
            pltpu.VMEM((6 * SUB, jobs), BF),
            pltpu.VMEM((6 * SUB, n_rep * LANES), F32),
            pltpu.VMEM((n_rep, 3 * SUB, LANES), F32),
            pltpu.VMEM((n_rep, 3 * SUB, LANES), F32),
            pltpu.VMEM((CAP * LANES, LANES), BF),
            pltpu.VMEM((CAP * LANES, LANES), BF),
            pltpu.VMEM((8 * PART, CAP * LANES), BF),
            pltpu.VMEM((5, LANES, LANES), F32),
            pltpu.VMEM((5, LANES, LANES), F32),
            pltpu.VMEM((n_rep, 9 * PART, tracts), F32),
            dma((2, n_rep - 1)),
            dma((2, n_rep - 1)),
            dma((5,)),
            dma((5,)),
            dma((2, n_rep - 1)),
            dma((2, n_rep - 1)),
        ],
        compiler_params=pltpu.CompilerParams(
            collective_id=0, has_side_effects=True, vmem_limit_bytes=40 * 2**20
        ),
        name="newton",
    )(
        base.reshape(n, LANES),
        job_res.reshape(n, LANES),
        job_slot.reshape(n, LANES),
        job_cell.reshape(n, LANES),
        needed.reshape(1, LANES),
        lam_res,
        lam_work,
        target_res,
        target_work,
    )
    out = jax.ShapeDtypeStruct((cells, tracts), F32)

    def fast():
        return tuple(
            pl.pallas_call(
                hand_out, out_shape=[out] * 4, in_specs=[vmem], out_specs=[vmem] * 4, name="finish"
            )(stack)
        )

    return lax.cond(flag[0, 0] == 0, fast, lambda: tuple(general(*args)))


def solution(mesh):
    in_specs = (
        P(("geo", "rep")),
        P(("geo", "rep")),
        P(("geo", "rep")),
        P(("geo", "rep")),
        P("geo", None, None),
        P(None, "geo"),
        P(None, "geo"),
        P(None, "geo"),
        P(None, "geo"),
    )
    out_specs = (P(None, "geo"), P(None, "geo"), P(None, "geo"), P(None, "geo"))
    work = functools.partial(body, mesh.shape["geo"], mesh.shape["rep"])
    return jax.shard_map(work, mesh=mesh, in_specs=in_specs, out_specs=out_specs, check_vma=False)
```

```python
import functools

import jax
import jax.numpy as jnp
from jax import lax
from jax.experimental import pallas as pl
from jax.experimental.pallas import tpu as pltpu
from jax.sharding import PartitionSpec as P

BLK = 32
ITERS = 3
RIDGE = 0.5
MESH = pl.DeviceIdType.MESH
LANES = 128
PART = 8
SUB = 24
CAP = 48
STEEP = 128.0
FLAT = 1e-3
BF = jnp.bfloat16
F32 = jnp.float32


def gather(table, index, rows):
    high = index >> 7
    low = index & 127
    out = jnp.zeros(index.shape, F32)
    for row in range(rows):
        for half in range(2):
            line = table[row : row + 1, half * LANES : (half + 1) * LANES]
            line = jnp.broadcast_to(line, index.shape)
            out = jnp.where(high == 2 * row + half, jnp.take_along_axis(line, low, axis=1), out)
    return out


def split(x):
    high = x.astype(BF).astype(F32)
    return high, x - high


def newton_kernel(
    n_geo, n_rep, *refs
):
    operands, (o_all, o_flag), held = refs[:9], refs[9:11], refs[11:20]
    base, res, slot, cell, needed, lam_res, lam_work, t_res, t_work = held
    run_newton(
        n_geo, n_rep, operands, held, base, res, slot, cell, needed, lam_res, lam_work, t_res,
        t_work, o_all, o_flag, *refs[20:]
    )


def run_newton(
    n_geo, n_rep, operands, held, base, res, slot, cell, needed, lam_res, lam_work, t_res, t_work,
    o_all, o_flag, held_sem, wide, ohp, pre, fields, place, xsend, xlist, oht_r, oht_w, left, send, recv, xbuf,
    list_send_sem, list_recv_sem, send_sem, recv_sem, xsend_sem, xrecv_sem,
):
    g, r = lax.axis_index("geo"), lax.axis_index("rep")
    barrier = pltpu.get_barrier_semaphore()

    loads = []
    for k, (source, target) in enumerate(zip(operands, held)):
        load = pltpu.make_async_copy(source, target, held_sem.at[k])
        load.start()
        loads.append(load)

    depth = n_geo // 16
    z, y, core = g // 16, lax.rem(g // 2, 8), lax.rem(g, 2)
    lows = [
        lax.rem(y + d, 8) * 2 + lax.rem(core + e, 2)
        for d in (4, 3, 5, 2, 6, 1, 7, 0)
        for e in (1, 0)
    ]

    def each_peer(act):
        def plane(j, carry):
            high = lax.rem(z + j + 3, depth) * 16
            for low in lows[:-1]:
                act(high + low)
            return carry

        lax.fori_loop(0, depth, plane, 0)
        for d in range(1, depth):
            act(lax.rem(z + d, depth) * 16 + lows[-1])

    each_peer(
        lambda peer: pl.semaphore_signal(barrier, inc=1, device_id=(peer, r), device_id_type=MESH)
    )
    for i in range(1, n_rep):
        pl.semaphore_signal(
            barrier, inc=1, device_id=(g, lax.rem(r + i, n_rep)), device_id_type=MESH
        )

    for load in loads:
        load.wait()
    cells = lam_res.shape[0]
    c = cell[...]
    s = slot[...]
    p = s >> 5
    block = jnp.take_along_axis(jnp.broadcast_to(needed[...], s.shape), p, axis=1)
    u_all = base[...] * jnp.exp(gather(lam_res[...], c * 256 + res[...], cells))
    bucket = (c >> 3) * LANES + p
    chunks = base.shape[0] // 2
    peers = lax.broadcasted_iota(jnp.int32, (n_rep * LANES, 2 * LANES), 0)

    def pair(x, k):
        return jnp.concatenate([x[2 * k : 2 * k + 1, :], x[2 * k + 1 : 2 * k + 2, :]], axis=1)

    before = lax.broadcasted_iota(jnp.int32, (2 * LANES, 2 * LANES), 0)
    after = lax.broadcasted_iota(jnp.int32, (2 * LANES, 2 * LANES), 1)
    upto = jnp.where(before <= after, 1.0, 0.0).astype(BF)
    for k in range(chunks):
        span = slice(k * 256, (k + 1) * 256)
        ohp[:, span] = jnp.where(pair(bucket, k) == peers, 1.0, 0.0).astype(BF)
    for k in range(chunks):
        span = slice(k * 256, (k + 1) * 256)
        pre[:, span] = jnp.dot(ohp[:, span], upto, preferred_element_type=F32)
    u_1 = u_all.astype(BF).astype(F32)
    u_2 = (u_all - u_1).astype(BF).astype(F32)
    kinds = (
        u_1,
        u_2,
        u_all - u_1 - u_2,
        (c & (PART - 1)).astype(F32),
        (block * BLK + (s & (BLK - 1))).astype(F32),
        res[...].astype(F32),
    )
    steps = lax.broadcasted_iota(jnp.int32, (SUB, 256), 0).astype(F32)
    so_far = jnp.zeros((n_rep * LANES, 1), F32)
    for k in range(chunks):
        span = slice(k * 256, (k + 1) * 256)
        here = pre[:, span]
        rank = jnp.sum(ohp[:, span].astype(F32) * (here + so_far), axis=0, keepdims=True) - 1.0
        so_far = so_far + here[:, 255:256]
        spot = rank == steps
        for f, kind in enumerate(kinds):
            fields[f * SUB : (f + 1) * SUB, span] = jnp.where(spot, pair(kind, k), 0.0).astype(BF)
    most = jnp.max(so_far)
    place[...] = lax.dot_general(
        fields[...], ohp[...], (((1,), (1,)), ((), ())), preferred_element_type=F32
    )
    for q in range(n_rep):
        lists = [
            place[f * SUB : (f + 1) * SUB, q * LANES : (q + 1) * LANES] for f in range(len(kinds))
        ]
        xsend[q, 0:SUB, :] = lists[0] + lists[1] + lists[2]
        xsend[q, SUB : 2 * SUB, :] = lists[3] * 256.0 + lists[4]
        xsend[q, 2 * SUB : 3 * SUB, :] = lists[3] * 256.0 + lists[5]
    for k, table in enumerate((lam_work, t_res, t_work)):
        wide[k] = jnp.zeros(wide.shape[1:], F32)
        wide[k, 0:cells, :] = table[...]
    mine = pl.ds(pl.multiple_of(r * PART, PART), PART)
    parts = [wide[k, mine, :] for k in range(3)]
    pl.semaphore_wait(barrier, n_geo - 1 + n_rep - 1)

    around = sorted(range(1, n_rep), key=lambda i: -min(i, n_rep - i))

    def swap(lo, hi, which):
        copies = []
        for i in around:
            other = lax.rem(r + i, n_rep)
            copy = pltpu.make_async_remote_copy(
                src_ref=xsend.at[other, pl.ds(lo, hi - lo)],
                dst_ref=xlist.at[r, pl.ds(lo, hi - lo)],
                send_sem=list_send_sem.at[which, i - 1],
                recv_sem=list_recv_sem.at[which, i - 1],
                device_id=(g, other),
                device_id_type=MESH,
            )
            copy.start()
            copies.append(copy)
        return copies

    lists_now = swap(0, 2 * SUB, 0)
    lists_later = swap(2 * SUB, 3 * SUB, 1)
    xlist[r] = xsend[r]
    for copy in lists_now:
        copy.wait_recv()

    counts = [
        jnp.sum(jnp.where(xlist[q, 0:SUB, :] > 0.0, 1, 0), axis=0, keepdims=True)
        for q in range(n_rep)
    ]

    def merge(field):
        total = jnp.zeros((CAP, LANES), F32)
        offset = jnp.zeros((1, LANES), jnp.int32)
        for q in range(n_rep):
            x = xlist[q, field * SUB : (field + 1) * SUB, :]
            x = jnp.concatenate([x, jnp.zeros((CAP - SUB, LANES), F32)], axis=0)
            if q:
                for bit in range(6):
                    width = 1 << bit
                    gap = jnp.zeros((width, LANES), F32)
                    down = jnp.concatenate([gap, x[: CAP - width]], axis=0)
                    x = jnp.where((offset >> bit) & 1 == 1, down, x)
            total = total + x
            offset = offset + counts[q]
        return total

    total = sum(counts[1:], counts[0])
    crowded = jnp.where(jnp.logical_or(most > SUB, total > CAP), 1.0, 0.0)

    pad = jnp.zeros((LANES - 2 * CAP, LANES), F32)

    def launch(k, first, second):
        whole = jnp.concatenate([first, second, pad], axis=0)
        send[k] = jnp.transpose(whole)

        each_peer(
            lambda peer: pltpu.make_async_remote_copy(
                src_ref=send.at[k, pl.ds(peer, 1)],
                dst_ref=recv.at[k, pl.ds(g, 1)],
                send_sem=send_sem.at[k],
                recv_sem=recv_sem.at[k],
                device_id=(peer, r),
                device_id_type=MESH,
            ).start()
        )
        recv[k, pl.ds(g, 1), :] = send[k, pl.ds(g, 1), :]

    def everything(k):
        return pltpu.make_async_remote_copy(
            src_ref=send.at[k, pl.ds(0, n_geo - 1)],
            dst_ref=recv.at[k, pl.ds(0, n_geo - 1)],
            send_sem=send_sem.at[k],
            recv_sem=recv_sem.at[k],
            device_id=(g, r),
            device_id_type=MESH,
        )

    def arrive(k):
        everything(k).wait_recv()
        return jnp.transpose(recv[k])

    def over(x):
        x = x.astype(F32)
        return jnp.transpose(jnp.concatenate([x, jnp.zeros((LANES - CAP, LANES), F32)], axis=0))

    tracts = lax.broadcasted_iota(jnp.int32, (LANES, LANES), 1).astype(F32)

    def columns(oht, numbers):
        for k in range(CAP):
            hot = jnp.where(numbers[:, k : k + 1] == tracts, 1.0, 0.0)
            oht[k * LANES : (k + 1) * LANES, :] = hot.astype(BF)

    lines = lax.broadcasted_iota(jnp.int32, (2 * PART, LANES), 0)

    def line_of(index):
        return (index >> 8) + PART * ((index >> 7) & 1)

    def scatter(values, line, oht):
        pieces = [piece for value in values for piece in split(value)]
        high = 2 * PART
        for k in range(CAP):
            mine = line[k : k + 1, :] == lines
            stack = [jnp.where(mine, piece[k : k + 1, :], 0.0) for piece in pieces]
            left[0 : high * len(pieces), k * LANES : (k + 1) * LANES] = jnp.concatenate(
                stack, axis=0
            ).astype(BF)
        out = jnp.dot(left[0 : high * len(pieces), :], oht[...], preferred_element_type=F32)
        sums = [
            out[2 * v * high : (2 * v + 1) * high] + out[(2 * v + 1) * high : (2 * v + 2) * high]
            for v in range(len(values))
        ]
        return [jnp.concatenate([x[:PART], x[PART:]], axis=1) for x in sums]

    launch(0, merge(0), merge(1))
    for copy in lists_later:
        copy.wait_recv()
    home_g = merge(2).astype(jnp.int32)
    line_g = line_of(home_g)
    columns(oht_r, over(home_g & 127))

    flat = arrive(0)
    u_o = flat[0:CAP]
    work_o = flat[CAP : 2 * CAP].astype(jnp.int32)
    line_o = line_of(work_o)
    columns(oht_w, over(work_o & 127))
    w_o = u_o * gather(jnp.exp(parts[0]), work_o, PART)
    [sum_w] = scatter([w_o], line_o, oht_w)
    diag_w = sum_w + RIDGE
    b0 = parts[2] - sum_w
    launch(1, w_o, gather(b0, work_o, PART))

    flat = arrive(1)
    w_g = flat[0:CAP]
    sum_r, bb0 = scatter([w_g, w_g * flat[CAP : 2 * CAP]], line_g, oht_r)
    diag_r = sum_r + RIDGE
    a0 = parts[1] - sum_r
    a1 = diag_r * a0 + bb0
    launch(2, w_g * gather(a0, home_g, PART), w_g * gather(a1, home_g, PART))

    flat = arrive(2)
    ba0, ba1 = scatter([flat[0:CAP], flat[CAP : 2 * CAP]], line_o, oht_w)
    b1 = diag_w * b0 + ba0
    b2 = diag_w * b1 + ba1
    launch(3, w_o * gather(b1, work_o, PART), w_o * gather(b2, work_o, PART))

    flat = arrive(3)
    bb1, bb2 = scatter([flat[0:CAP], flat[CAP : 2 * CAP]], line_g, oht_r)
    a2 = diag_r * a1 + bb1
    a3 = diag_r * a2 + bb2

    def line(x):
        x = x[:, 0:LANES] + x[:, LANES : 2 * LANES]
        return jnp.sum(x, axis=0, keepdims=True)

    steep = jnp.maximum(sum_r, sum_w)
    steep = jnp.max(jnp.maximum(steep[:, :LANES], steep[:, LANES:]), axis=0, keepdims=True)
    bad = jnp.where(steep > STEEP, 1.0, crowded)
    table = jnp.concatenate(
        [
            line(a0 * a0 + b0 * b0),
            line(a0 * a1 + b0 * b1),
            line(a1 * a1 + b1 * b1),
            line(a1 * a2 + b1 * b2),
            line(a2 * a2 + b2 * b2),
            line(a2 * (a3 + bb2) + diag_w * b2 * b2),
            bad,
            jnp.zeros((1, LANES), F32),
        ],
        axis=0,
    )
    table = jnp.broadcast_to(jnp.sum(table, axis=1, keepdims=True), (8, LANES))
    launch(
        4,
        w_g * gather(a2, home_g, PART),
        jnp.concatenate([table, jnp.zeros((CAP - 8, LANES), F32)], axis=0),
    )

    early = 7 * PART
    for v, vector in enumerate((a0, a1, a2, a3, b0, b1, b2)):
        xbuf[r, v * PART : (v + 1) * PART, :] = vector

    def across(lo, hi, which):
        copies = []
        for i in around:
            copy = pltpu.make_async_remote_copy(
                src_ref=xbuf.at[r, pl.ds(lo, hi - lo)],
                dst_ref=xbuf.at[r, pl.ds(lo, hi - lo)],
                send_sem=xsend_sem.at[which, i - 1],
                recv_sem=xrecv_sem.at[which, i - 1],
                device_id=(g, lax.rem(r + i, n_rep)),
                device_id_type=MESH,
            )
            copy.start()
            copies.append(copy)
        return copies

    first = across(0, early, 0)

    flat = arrive(4)
    [ba2] = scatter([flat[0:CAP]], line_o, oht_w)
    b3 = diag_w * b2 + ba2
    xbuf[r, early : early + PART, :] = b3
    xbuf[r, early + PART : early + 2 * PART, :] = jnp.broadcast_to(
        jnp.sum(flat[CAP : CAP + 8], axis=1, keepdims=True), (8, 256)
    )
    last = across(early, early + 2 * PART, 1)
    for copy in first + last:
        copy.wait_recv()

    sums = xbuf[0, early + PART : early + 2 * PART, :]
    for q in range(1, n_rep):
        sums = sums + xbuf[q, early + PART : early + 2 * PART, :]
    m = [sums[i : i + 1, :] for i in range(7)]

    def form(x, shift):
        n = len(x)
        total = None
        for s in range(2 * n - 1):
            part = None
            for i in range(max(0, s - n + 1), min(n - 1, s) + 1):
                term = x[i] * x[s - i]
                part = term if part is None else part + term
            part = part * m[s + shift]
            total = part if total is None else total + part
        return total

    one = jnp.ones((1, 256), F32)
    rc, pc, xc = [one], [one], []
    norm = m[0]
    for turn in range(ITERS):
        alpha = norm / form(pc, 1)
        xc = [x + alpha * p for x, p in zip(xc, pc)] + [alpha * pc[-1]]
        image = [-alpha * p for p in pc]
        rc = [rc[0]] + [x + y for x, y in zip(rc[1:], image[:-1])] + [image[-1]]
        if turn < ITERS - 1:
            new = form(rc, 0)
            beta = new / norm
            pc = [x + beta * p for x, p in zip(rc[:-1], pc)] + [rc[-1]]
            norm = new
    good = jnp.logical_and(m[6] == 0.0, norm > FLAT * m[0])
    o_flag[0, 0] = jnp.max(jnp.where(good, 0, 1))
    for q in range(n_rep):
        lo = q * PART
        for side in range(2):
            k = [xbuf[q, (4 * side + i) * PART : (4 * side + i + 1) * PART, :] for i in range(4)]
            o_all[side, lo : lo + PART, :] = xc[0] * k[0] + xc[1] * k[1] + xc[2] * k[2]
            o_all[2 + side, lo : lo + PART, :] = k[0] + rc[1] * k[1] + rc[2] * k[2] + rc[3] * k[3]
    for copy in lists_now + lists_later + first + last:
        copy.wait_send()
    for k in range(5):
        everything(k).wait_send()


def hand_out(stack, *outs):
    for k, out in enumerate(outs):
        out[...] = stack[k, 0 : out.shape[0], :]


def general(base, job_res, job_slot, job_cell, needed, lam_res, lam_work, target_res, target_work):
    cells, tracts_dev = lam_res.shape
    blocks_dev = tracts_dev // BLK
    requests = lax.all_to_all(needed[0], "geo", split_axis=0, concat_axis=0, tiled=True)
    sources, listed = requests.shape
    hot = requests[:, :, None] == jnp.arange(blocks_dev, dtype=jnp.int32)[None, None, :]
    onehot = hot.astype(jnp.float32)
    slot_shape = (sources, listed, cells, BLK)
    slot_count = sources * listed * cells * BLK
    res_index = job_cell * tracts_dev + job_res
    work_index = (job_slot // BLK * cells + job_cell) * BLK + job_slot % BLK

    def serve(table):
        blocks = table.reshape(cells, blocks_dev, BLK).transpose(1, 0, 2)
        out = jnp.zeros(slot_shape, jnp.float32)
        for b in range(blocks_dev):
            out = jnp.where(hot[:, :, b, None, None], blocks[b][None, None], out)
        return out

    def pick(fetched):
        return fetched.reshape(-1)[work_index]

    def fold(arrived):
        return jnp.einsum("skb,skcx->cbx", onehot, arrived, precision=lax.Precision.HIGHEST)

    def totals(values):
        res_part = jax.ops.segment_sum(values, res_index, num_segments=cells * tracts_dev).reshape(
            cells, tracts_dev
        )
        work_part = jax.ops.segment_sum(values, work_index, num_segments=slot_count).reshape(
            slot_shape
        )
        arrived = lax.all_to_all(work_part, "geo", split_axis=0, concat_axis=0, tiled=True)
        folded = fold(arrived)
        return lax.psum((res_part, folded.reshape(cells, tracts_dev)), "rep")

    def squares(part_res, part_work):
        local = jnp.sum(part_res * part_res) + jnp.sum(part_work * part_work)
        return lax.psum(local, "geo")

    def fetch(table):
        return lax.all_to_all(serve(table), "geo", split_axis=0, concat_axis=0, tiled=True)

    weight = base * jnp.exp(lam_res.reshape(-1)[res_index] + pick(fetch(lam_work)))
    total_res, total_work = totals(weight)
    resid_res = -(total_res - target_res)
    resid_work = -(total_work - target_work)
    zero = jnp.zeros_like(resid_res)
    norm = squares(resid_res, resid_work)

    def turn(_, state):
        step_res, step_work, resid_res, resid_work, dir_res, dir_work, norm_now = state
        along = dir_res.reshape(-1)[res_index] + pick(fetch(dir_work))
        image_res, image_work = totals(weight * along)
        image_res = image_res + RIDGE * dir_res
        image_work = image_work + RIDGE * dir_work
        local_curv = jnp.sum(dir_res * image_res) + jnp.sum(dir_work * image_work)
        alpha = norm_now / lax.psum(local_curv, "geo")
        step_res = step_res + alpha * dir_res
        step_work = step_work + alpha * dir_work
        resid_res = resid_res - alpha * image_res
        resid_work = resid_work - alpha * image_work
        norm_next = squares(resid_res, resid_work)
        dir_res = resid_res + norm_next / norm_now * dir_res
        dir_work = resid_work + norm_next / norm_now * dir_work
        return step_res, step_work, resid_res, resid_work, dir_res, dir_work, norm_next

    state = (zero, zero, resid_res, resid_work, resid_res, resid_work, norm)
    return lax.fori_loop(0, ITERS, turn, state)[:4]


def body(n_geo, n_rep, *args):
    base, job_res, job_slot, job_cell, needed, lam_res, lam_work, target_res, target_work = args
    n = base.shape[0] // LANES
    cells, tracts = lam_res.shape
    vmem = pl.BlockSpec(memory_space=pltpu.VMEM)
    dma = pltpu.SemaphoreType.DMA
    operands = [x.reshape(n, LANES) for x in (base, job_res, job_slot, job_cell)]
    operands += [needed.reshape(1, LANES), lam_res, lam_work, target_res, target_work]
    smem = pl.BlockSpec(memory_space=pltpu.SMEM)
    jobs = n * LANES
    stack, flag = pl.pallas_call(
        functools.partial(newton_kernel, n_geo, n_rep),
        out_shape=[
            jax.ShapeDtypeStruct((4, n_rep * PART, tracts), F32),
            jax.ShapeDtypeStruct((1, 1), jnp.int32),
        ],
        in_specs=[pl.BlockSpec(memory_space=pltpu.HBM)] * 9,
        out_specs=[vmem, smem],
        scratch_shapes=[pltpu.VMEM(x.shape, x.dtype) for x in operands]
        + [
            dma((len(operands),)),
            pltpu.VMEM((3, n_rep * PART, tracts), F32),
            pltpu.VMEM((n_rep * LANES, jobs), BF),
            pltpu.VMEM((n_rep * LANES, jobs), F32),
            pltpu.VMEM((6 * SUB, jobs), BF),
            pltpu.VMEM((6 * SUB, n_rep * LANES), F32),
            pltpu.VMEM((n_rep, 3 * SUB, LANES), F32),
            pltpu.VMEM((n_rep, 3 * SUB, LANES), F32),
            pltpu.VMEM((CAP * LANES, LANES), BF),
            pltpu.VMEM((CAP * LANES, LANES), BF),
            pltpu.VMEM((8 * PART, CAP * LANES), BF),
            pltpu.VMEM((5, LANES, LANES), F32),
            pltpu.VMEM((5, LANES, LANES), F32),
            pltpu.VMEM((n_rep, 9 * PART, tracts), F32),
            dma((2, n_rep - 1)),
            dma((2, n_rep - 1)),
            dma((5,)),
            dma((5,)),
            dma((2, n_rep - 1)),
            dma((2, n_rep - 1)),
        ],
        compiler_params=pltpu.CompilerParams(
            collective_id=0, has_side_effects=True, vmem_limit_bytes=40 * 2**20
        ),
        name="newton",
    )(*operands)
    out = jax.ShapeDtypeStruct((cells, tracts), F32)

    def fast():
        return tuple(
            pl.pallas_call(
                hand_out, out_shape=[out] * 4, in_specs=[vmem], out_specs=[vmem] * 4, name="finish"
            )(stack)
        )

    return lax.cond(flag[0, 0] == 0, fast, lambda: tuple(general(*args)))


def solution(mesh):
    in_specs = (
        P(("geo", "rep")),
        P(("geo", "rep")),
        P(("geo", "rep")),
        P(("geo", "rep")),
        P("geo", None, None),
        P(None, "geo"),
        P(None, "geo"),
        P(None, "geo"),
        P(None, "geo"),
    )
    out_specs = (P(None, "geo"), P(None, "geo"), P(None, "geo"), P(None, "geo"))
    work = functools.partial(body, mesh.shape["geo"], mesh.shape["rep"])
    return jax.shard_map(work, mesh=mesh, in_specs=in_specs, out_specs=out_specs, check_vma=False)
```
